32 devices in a mesh: leaf: 8 (over y, x, core), rep: 4 (over z).
Axes of the slice: x: 2, y: 2, z: 4, core: 2. Of those that a mesh axis runs over, the one named last changes fastest.
Arguments:
- local_right: float32 [8, 4, 2048, 128], P('leaf', 'rep'), may hold values from -6 to 6
- local_inverse: bfloat16 [8, 4, 16, 128, 128], P('leaf', 'rep'), may hold values from -1 to 1.4, as said below
- local_below: bfloat16 [8, 4, 15, 128, 128], P('leaf', 'rep'), may hold values from -0.5 to 0.5
- local_parent: int32 [8, 4, 15], P('leaf', 'rep'), may hold values from 1 to 15, as said below
- local_coupling: bfloat16 [8, 4, 3, 384, 2048], P('leaf', 'rep'), may hold values from -0.1 to 0.1
- separator_right: float32 [7, 384, 128], replicated, may hold values from -6 to 6
- separator_inverse: bfloat16 [7, 3, 128, 128], replicated, may hold values from -1 to 1.4, as said below
- separator_lower: bfloat16 [7, 384, 384], replicated, may hold values from -0.3125 to 0.3125
- parent_coupling: bfloat16 [6, 384, 384], replicated, may hold values from -0.3125 to 0.3125
Outputs:
- local_solution: float32 [8, 4, 2048, 128], P('leaf', 'rep')
- separator_solution: float32 [8, 3, 384, 128], P('leaf')
The draws below stay inside these ranges and needn't reach their ends.
Inputs may be any that keep to these rules, and one draw needn't show every extreme that they name: `local_parent`: entry k of a device's list is larger than k. `local_inverse`: every block is lower triangular. `separator_inverse`: every block is lower triangular.
All inputs are finite; a program needn't handle non-finite values.
Results may differ from the reference program's by a relative error of at most 0.035.
Values sent between devices are 32-bit elements; how exact they have to be, the bound alone decides.
A program may use at most 128 MiB of HBM per device.

```python
import math
import jax
import jax.numpy as jnp
from jax import lax

NB = 128
R = 128
LB = 16
SB = 3
ROWS = 2048
S = 384
LEV = 3
NSEP = 7
N_LEAF = 8
N_REP = 4


def triangle_blocks(key, leading):
    first_key, second_key = jax.random.split(key)
    shape = leading + (NB, NB)
    row_index = lax.broadcasted_iota(jnp.int32, shape, len(shape) - 2)
    col_index = lax.broadcasted_iota(jnp.int32, shape, len(shape) - 1)
    diagonal = jax.random.uniform(first_key, shape, jnp.float32, 0.6, 1.4)
    offdiag = jax.random.normal(second_key, shape, jnp.float32) * (0.6 / math.sqrt(NB))
    offdiag = jnp.clip(offdiag, -0.9, 0.9)
    result = jnp.where(row_index == col_index, diagonal, jnp.where(row_index > col_index, offdiag, 0.0))
    return result.astype(jnp.bfloat16)


def draw_local_inverse(key, part):
    return triangle_blocks(key, (N_LEAF, N_REP, LB))


def draw_separator_inverse(key, part):
    return triangle_blocks(key, (NSEP, SB))


def draw_local_parent(key, part):
    shape = (N_LEAF, N_REP, LB - 1)
    index = lax.broadcasted_iota(jnp.int32, shape, 2)
    randbits = jax.random.randint(key, shape, 0, 1 << 30, dtype=jnp.int32)
    return (index + 1 + randbits % (LB - 1 - index)).astype(jnp.int32)


def draw_local_coupling(key, part):
    shape = (N_LEAF, N_REP, LEV, S, ROWS)
    height = lax.broadcasted_iota(jnp.float32, (1, 1, LEV, 1, 1), 2)
    scaling = jnp.exp2(-(height + 1.0) * 0.5) / math.sqrt(ROWS * N_REP)
    values = jnp.clip(jax.random.normal(key, shape, jnp.float32), -8.0, 8.0) * scaling
    values = jnp.clip(values, -0.09375, 0.09375)
    return values.astype(jnp.bfloat16)


def shard_levels(own_key, extent, shards, low, largest):
    def one(dim, shards_of):
        steps = jax.random.uniform(jax.random.fold_in(jax.random.fold_in(own_key, 6), dim), (shards_of,), jnp.float32, low / len(shards), largest / len(shards))
        return jnp.repeat(jnp.exp(steps), extent[dim] // shards_of).reshape((-1,) + (1,) * (len(extent) - dim - 1))

    factor_of = one(*shards[0])
    for cut in shards[1:]:
        factor_of = factor_of * one(*cut)
    return factor_of


def scatter_about(key, shape, deviation, bound, pieces=(), kind=jnp.bfloat16):
    gain = shard_levels(key, shape, pieces, -0.22, 0.18) if pieces else 1.0
    entries = jax.random.normal(key, shape, jnp.float32) * deviation * gain
    return jnp.minimum(jnp.maximum(entries, -bound), bound).astype(kind)


def setup_inputs(seed: int = 0) -> dict:
    streams_of = jax.random.split(jax.random.key(seed), 10)
    local_right = scatter_about(streams_of[0], (N_LEAF, N_REP, ROWS, R), 1.0, 6.0, ((0, 8), (1, 4)), jnp.float32)
    local_inverse = draw_local_inverse(jax.random.fold_in(streams_of[9], 71), 0)
    local_below = scatter_about(streams_of[2], (N_LEAF, N_REP, LB - 1, NB, NB), NB ** -0.5, 0.5, ((0, 8), (1, 4)))
    local_parent = draw_local_parent(jax.random.fold_in(streams_of[9], 71), 0)
    local_coupling = draw_local_coupling(jax.random.fold_in(streams_of[9], 71), 0)
    separator_right = scatter_about(streams_of[5], (NSEP, S, R), 1.0, 6.0, (), jnp.float32)
    separator_inverse = draw_separator_inverse(jax.random.fold_in(streams_of[9], 71), 0)
    separator_lower = scatter_about(streams_of[7], (NSEP, S, S), S ** -0.5, 0.3125)
    parent_coupling = scatter_about(streams_of[8], (NSEP - 1, S, S), S ** -0.5, 0.3125)
    return {"local_right": local_right, "local_inverse": local_inverse, "local_below": local_below, "local_parent": local_parent, "local_coupling": local_coupling, "separator_right": separator_right, "separator_inverse": separator_inverse, "separator_lower": separator_lower, "parent_coupling": parent_coupling}


def apply_lower(matrix, vector):
    return jnp.dot(matrix, vector.astype(jnp.bfloat16), preferred_element_type=jnp.float32)


def apply_upper(matrix, vector):
    return jnp.dot(matrix.T, vector.astype(jnp.bfloat16), preferred_element_type=jnp.float32)


def block_lookup_tables(below, parents):
    targets = jnp.concatenate([parents.astype(jnp.int32), jnp.full((1,), LB, jnp.int32)]).astype(jnp.int32)
    padded = jnp.concatenate([below, jnp.zeros((1, NB, NB), below.dtype)], axis=0)
    orders = jnp.arange(LB, dtype=jnp.int32)
    return targets, padded, orders


def local_forward(righthand, inverse, below, parents):
    columns = righthand.shape[1]
    blocks = righthand.reshape(LB, NB, columns)
    targets, padded, orders = block_lookup_tables(below, parents)

    def advance(carried, items):
        current, inv_block, low_block, target, number = items
        result = apply_lower(inv_block, current - carried[number])
        carried = carried.at[target].add(apply_lower(low_block, result))
        return carried, result

    start = jnp.zeros((LB + 1, NB, columns), jnp.float32)
    _, results = lax.scan(advance, start, (blocks, inverse, padded, targets, orders))
    return results.reshape(LB * NB, columns)


def local_backward(forward, update_terms, inverse, below, parents):
    columns = forward.shape[1]
    remains = (forward - update_terms).reshape(LB, NB, columns)
    targets, padded, orders = block_lookup_tables(below, parents)

    def retreat(carried, items):
        current, inv_block, low_block, target, number = items
        result = apply_upper(inv_block, current - apply_upper(low_block, carried[target]))
        carried = carried.at[number].set(result.astype(jnp.bfloat16))
        return carried, result

    start = jnp.zeros((LB + 1, NB, columns), jnp.bfloat16)
    _, results = lax.scan(retreat, start, (remains, inverse, padded, targets, orders), reverse=True)
    return results.reshape(LB * NB, columns)


def separator_forward(righthand, inverse, lowerpart):
    solved = []
    rounded = []
    for position in range(SB):
        current = righthand[position * NB:(position + 1) * NB]
        if position > 0:
            earlier = jnp.concatenate(rounded, axis=0)
            current = current - jnp.dot(lowerpart[position * NB:(position + 1) * NB, :position * NB], earlier, preferred_element_type=jnp.float32)
        result = apply_lower(inverse[position], current)
        solved.append(result)
        rounded.append(result.astype(jnp.bfloat16))
    return jnp.concatenate(solved, axis=0), jnp.concatenate(rounded, axis=0)


def separator_backward(righthand, inverse, lowerpart):
    solved = [None] * SB
    rounded = [None] * SB
    for position in reversed(range(SB)):
        current = righthand[position * NB:(position + 1) * NB]
        if position < SB - 1:
            later = jnp.concatenate(rounded[position + 1:], axis=0)
            current = current - apply_upper(lowerpart[(position + 1) * NB:, position * NB:(position + 1) * NB], later)
        result = apply_upper(inverse[position], current)
        solved[position] = result
        rounded[position] = result.astype(jnp.bfloat16)
    return jnp.concatenate(solved, axis=0), jnp.concatenate(rounded, axis=0)


def reference(local_right, local_inverse, local_below, local_parent, local_coupling, separator_right, separator_inverse, separator_lower, parent_coupling):
    members_all = N_LEAF * N_REP

    def flatten(array):
        return array.reshape((members_all,) + array.shape[2:])

    forward = jax.vmap(local_forward)(flatten(local_right), flatten(local_inverse), flatten(local_below), flatten(local_parent))

    def partial_sums(items):
        coupling_matrix, values = items
        rounded = values.astype(jnp.bfloat16)
        return jnp.stack([jnp.dot(coupling_matrix[height], rounded, preferred_element_type=jnp.float32) for height in range(LEV)])

    partials = lax.map(partial_sums, (flatten(local_coupling), forward))
    leaf_totals = jnp.sum(partials.reshape(N_LEAF, N_REP, LEV, S, R), axis=1)

    forward_seps = {}
    rounded_seps = {}
    for height in range(1, LEV + 1):
        groups = N_LEAF >> height
        totals = jnp.sum(leaf_totals[:, height - 1].reshape(groups, 2 ** height, S, R), axis=1)
        solved = []
        rounded = []
        for member in range(groups):
            number = groups - 1 + member
            gathered = totals[member]
            if height > 1:
                for child in (2 * member, 2 * member + 1):
                    child_number = 2 * groups - 1 + child
                    gathered = gathered + jnp.dot(parent_coupling[child_number - 1], rounded_seps[height - 1][child], preferred_element_type=jnp.float32)
            result, result_round = separator_forward(separator_right[number] - gathered, separator_inverse[number], separator_lower[number])
            solved.append(result)
            rounded.append(result_round)
        forward_seps[height] = solved
        rounded_seps[height] = rounded

    back_seps = {}
    backward_pass_rounded = {}
    for height in range(LEV, 0, -1):
        groups = N_LEAF >> height
        solved = []
        rounded = []
        for member in range(groups):
            number = groups - 1 + member
            upward = forward_seps[height][member]
            if height < LEV:
                upward = upward - apply_upper(parent_coupling[number - 1], backward_pass_rounded[height + 1][member // 2])
            result, result_round = separator_backward(upward, separator_inverse[number], separator_lower[number])
            solved.append(result)
            rounded.append(result_round)
        back_seps[height] = jnp.stack(solved)
        backward_pass_rounded[height] = rounded

    copies = [jnp.repeat(back_seps[height], 2 ** height, axis=0) for height in range(1, LEV + 1)]
    separator_solution = jnp.stack(copies, axis=1)
    rounded_all = jnp.repeat(separator_solution.astype(jnp.bfloat16), N_REP, axis=0)

    def finish(items):
        coupling_matrix, rounded, values, inverse, below, parents = items
        update_terms = jnp.dot(coupling_matrix[0].T, rounded[0], preferred_element_type=jnp.float32)
        for height in range(1, LEV):
            update_terms = update_terms + jnp.dot(coupling_matrix[height].T, rounded[height], preferred_element_type=jnp.float32)
        return local_backward(values, update_terms, inverse, below, parents)

    local_solution = lax.map(finish, (flatten(local_coupling), rounded_all, forward, flatten(local_inverse), flatten(local_below), flatten(local_parent)))
    return local_solution.reshape(N_LEAF, N_REP, ROWS, R), separator_solution
```

```python
import functools

import jax
import jax.numpy as jnp
from jax import lax
from jax.experimental import pallas as pl
from jax.experimental.pallas import tpu as pltpu
from jax.sharding import PartitionSpec as P

F32 = jnp.float32
BF16 = jnp.bfloat16
MESH = pl.DeviceIdType.MESH


def nn(a, b):
    return jnp.dot(a, b, preferred_element_type=F32)


def nt(a, b):
    return lax.dot_general(a, b, (((1,), (1,)), ((), ())), preferred_element_type=F32)


def body(
    nleaf,
    nrep,
    par,
    right_hbm,
    inv_hbm,
    below_hbm,
    coup_hbm,
    sright_hbm,
    sinv_hbm,
    slow_hbm,
    pcoup_hbm,
    out_hbm,
    sep_hbm,
    right,
    inv,
    below,
    coup,
    sright,
    sinv,
    slow,
    pcoup,
    ctr,
    mfw,
    wbw,
    pj,
    x,
    eb,
    s0,
    tmat,
    qmat,
    umat,
    srt,
    part,
    pc,
    ph,
    zr,
    rem,
    lr,
    sol,
    out_v,
    sep_v,
    in_sem,
    core_s,
    core_r,
    z_s,
    z_r,
    l_s,
    l_r,
    g_s,
    g_r,
    gc_s,
    gc_r,
    out_sem,
):
    lev = coup.shape[0]
    lb = inv.shape[0]
    nb = inv.shape[1]
    s = coup.shape[1]
    sb = s // nb
    leaf = lax.axis_index("leaf")
    rep = lax.axis_index("rep")
    core = lax.rem(leaf, 2)
    mate = leaf + 1 - 2 * core

    def other_rep(d):
        return lax.rem(rep + d, nrep)

    def other_leaf(height):
        step = 1 << (height - 1)
        bit = lax.rem(leaf // step, 2)
        return leaf + step - 2 * step * bit

    numbers = [(nleaf >> h) - 1 + leaf // (1 << h) for h in range(1, lev + 1)]

    loads = [
        pltpu.make_async_copy(inv_hbm, inv, in_sem.at[0]),
        pltpu.make_async_copy(right_hbm, right, in_sem.at[1]),
        pltpu.make_async_copy(below_hbm, below, in_sem.at[2]),
        pltpu.make_async_copy(coup_hbm, coup, in_sem.at[3]),
    ]
    sep_loads = []
    for h in range(lev):
        n = numbers[h]
        base = 4 + 4 * h
        sep_loads.append(pltpu.make_async_copy(sinv_hbm.at[n], sinv.at[h], in_sem.at[base]))
        sep_loads.append(pltpu.make_async_copy(slow_hbm.at[n], slow.at[h], in_sem.at[base + 1]))
        sep_loads.append(pltpu.make_async_copy(sright_hbm.at[n], sright.at[h], in_sem.at[base + 2]))
        if h < lev - 1:
            sep_loads.append(
                pltpu.make_async_copy(pcoup_hbm.at[n - 1], pcoup.at[h], in_sem.at[base + 3])
            )
    for c in loads + sep_loads:
        c.start()

    barrier = pltpu.get_barrier_semaphore()
    peers = [(mate, rep)]
    peers += [(leaf, other_rep(d)) for d in range(1, nrep)]
    peers += [(other_leaf(h), rep) for h in range(2, lev + 1)]
    for peer in peers:
        pl.semaphore_signal(barrier, inc=1, device_id=peer, device_id_type=MESH)

    loads[0].wait()
    loads[1].wait()
    for k in range(lb):
        ctr[k] = nt(right[k].T.astype(BF16), inv[k])
    loads[2].wait()
    for k in range(lb - 1):
        mfw[k] = nn(inv[par[k]], below[k]).astype(BF16)
    for k in range(lb):
        acc = ctr[k]
        for j in range(k):
            acc = acc - jnp.where(par[j] == k, 1.0, 0.0) * pj[j]
        fb = acc.astype(BF16)
        x[k] = fb
        if k < lb - 1:
            pj[k] = nt(fb, mfw[k])

    pl.semaphore_wait(barrier, len(peers))
    loads[3].wait()
    fwd = jnp.concatenate([x[k] for k in range(lb)], axis=1)
    half = part.shape[2]
    core_copies = []
    for h in range(lev):
        prod = nt(fwd, coup[h])
        part[h, 0] = prod[:half]
        part[h, 1] = prod[half:]
        c = pltpu.make_async_remote_copy(
            src_ref=part.at[h, 1 - core],
            dst_ref=pc.at[h],
            send_sem=core_s.at[h],
            recv_sem=core_r.at[h],
            device_id=(mate, rep),
            device_id_type=MESH,
        )
        c.start()
        core_copies.append(c)

    for c in sep_loads:
        c.wait()

    def prepare(h):
        def low(i, j):
            return slow[h, i * nb : (i + 1) * nb, j * nb : (j + 1) * nb]

        t = {}
        for j in range(sb):
            t[j, j] = sinv[h, j]
            for i in range(j + 1, sb):
                total = nn(low(i, j), t[j, j])
                for m in range(j + 1, i):
                    total = total + nn(low(i, m), t[m, j])
                t[i, j] = (-nn(sinv[h, i], total.astype(BF16))).astype(BF16)
        for i in range(sb):
            for j in range(sb):
                block = t[i, j] if i >= j else jnp.zeros((nb, nb), BF16)
                tmat[h, i * nb : (i + 1) * nb, j * nb : (j + 1) * nb] = block
        full = tmat[h]
        umat[h] = lax.dot_general(
            full, full, (((0,), (0,)), ((), ())), preferred_element_type=F32
        ).astype(BF16)
        if h < lev - 1:
            qmat[h] = nn(pcoup[h], full).astype(BF16)
        srt[h] = sright[h].T.reshape(srt.shape[1:])

    prepare(0)

    rep_copies = []
    for h in range(lev):
        core_copies[h].wait()
        ph[h] = part[h, core].reshape(ph.shape[1:]) + pc[h].reshape(ph.shape[1:])
        row = []
        for d in range(1, nrep):
            c = pltpu.make_async_remote_copy(
                src_ref=ph.at[h, other_rep(d)],
                dst_ref=zr.at[h, d - 1],
                send_sem=z_s.at[h, d - 1],
                recv_sem=z_r.at[h, d - 1],
                device_id=(leaf, other_rep(d)),
                device_id_type=MESH,
            )
            c.start()
            row.append(c)
        rep_copies.append(row)

    for h in range(1, lev):
        prepare(h)

    for k in range(lb - 1):
        wbw[k, :nb] = inv[k]
        wbw[k, nb:] = (-nn(below[k], inv[k])).astype(BF16)

    def back_step(k):
        lanes = slice(k * nb, (k + 1) * nb)
        for g in range(lev + 1):
            if g == 0:
                rows = slice(0, x.shape[1])
                mine = x[k]
            else:
                rows = slice(x.shape[1] + (g - 1) * s, x.shape[1] + g * s)
                mine = coup[g - 1, :, lanes]
            if k == lb - 1:
                value = nn(mine, inv[k])
            else:
                value = nn(jnp.concatenate([mine, eb[par[k], rows]], axis=1), wbw[k])
            eb[k, rows] = value.astype(BF16)
            if g == 0:
                s0[k] = value

    steps = list(range(lb - 1, -1, -1))
    first = (lb * 5) // 8
    rest = lb - first
    for k in steps[:first]:
        back_step(k)
    steps = steps[first:]
    share = -(-rest // max(lev - 1, 1))

    slot = core * nrep + rep
    leaf_copies = {}

    def send_leaf(height, j):
        c = pltpu.make_async_remote_copy(
            src_ref=rem.at[height - 2, j],
            dst_ref=lr.at[height - 2, j],
            send_sem=l_s.at[height - 2, j],
            recv_sem=l_r.at[height - 2, j],
            device_id=(other_leaf(height), rep),
            device_id_type=MESH,
        )
        c.start()
        leaf_copies[height, j] = c

    def total_of(h):
        total = ph[h, rep]
        for c in rep_copies[h]:
            c.wait()
        for d in range(1, nrep):
            total = total + zr[h, d - 1]
        return total

    residues = []
    for height in range(1, lev + 1):
        h = height - 1
        if height == 1:
            now = total_of(0)
        else:
            leaf_copies[height, h].wait()
            now = rem[height - 2, h] + lr[height - 2, h]
        residue = (srt[h, slot] - now).astype(BF16)
        residues.append(residue)
        if height < lev:
            up = nt(residue, qmat[h])
            for j in range(height, lev):
                if height == 1:
                    value = total_of(j)
                else:
                    leaf_copies[height, j].wait()
                    value = rem[height - 2, j] + lr[height - 2, j]
                if j == height:
                    value = value + up
                rem[height - 1, j] = value
                send_leaf(height + 1, j)
            for k in steps[:share]:
                back_step(k)
            steps = steps[share:]

    gather_copies = []
    above = None
    for h in range(lev - 1, -1, -1):
        value = nn(residues[h], umat[h])
        if above is not None:
            value = value - nn(above, qmat[h])
        above = value.astype(BF16)
        sol[h, slot] = value
        row = []
        for d in range(1, nrep):
            c = pltpu.make_async_remote_copy(
                src_ref=sol.at[h, slot],
                dst_ref=sol.at[h, slot],
                send_sem=g_s.at[h, d - 1],
                recv_sem=g_r.at[h, d - 1],
                device_id=(leaf, other_rep(d)),
                device_id_type=MESH,
            )
            c.start()
            row.append(c)
        gather_copies.append(row)
    mate_copies = []
    for i, h in enumerate(range(lev - 1, -1, -1)):
        for c in gather_copies[i]:
            c.wait()
        c = pltpu.make_async_remote_copy(
            src_ref=sol.at[h, pl.ds(core * nrep, nrep)],
            dst_ref=sol.at[h, pl.ds(core * nrep, nrep)],
            send_sem=gc_s.at[h],
            recv_sem=gc_r.at[h],
            device_id=(mate, rep),
            device_id_type=MESH,
        )
        c.start()
        mate_copies.append(c)
    out_copies = []
    for i, h in enumerate(range(lev - 1, -1, -1)):
        mate_copies[i].wait()
        whole = sol[h].reshape(x.shape[1], s)
        rounded = whole.astype(BF16)
        rows = slice(x.shape[1] + h * s, x.shape[1] + (h + 1) * s)
        for k in range(lb):
            value = s0[k] - nn(rounded, eb[k, rows])
            if h > 0:
                s0[k] = value
            else:
                out_v[k] = value.T
                if k % 4 == 3:
                    part_k = pl.ds(k - 3, 4)
                    c = pltpu.make_async_copy(
                        out_v.at[part_k], out_hbm.at[part_k], out_sem.at[lev + k // 4]
                    )
                    c.start()
                    out_copies.append(c)
        sep_v[h] = whole.T
        c = pltpu.make_async_copy(sep_v.at[h], sep_hbm.at[h], out_sem.at[h])
        c.start()
        out_copies.append(c)
    for c in out_copies:
        c.wait()


def on_device(
    nleaf,
    nrep,
    local_right,
    local_inverse,
    local_below,
    local_parent,
    local_coupling,
    separator_right,
    separator_inverse,
    separator_lower,
    parent_coupling,
):
    _, _, lev, s, rows = local_coupling.shape
    lb, nb = local_inverse.shape[2:4]
    r = local_right.shape[3]
    w = r // (2 * nrep)
    sb = s // nb
    any_spec = pl.BlockSpec(memory_space=pl.ANY)
    scratch = [
        pltpu.VMEM((lb, nb, r), F32),
        pltpu.VMEM((lb, nb, nb), BF16),
        pltpu.VMEM((lb - 1, nb, nb), BF16),
        pltpu.VMEM((lev, s, rows), BF16),
        pltpu.VMEM((lev, s, r), F32),
        pltpu.VMEM((lev, sb, nb, nb), BF16),
        pltpu.VMEM((lev, s, s), BF16),
        pltpu.VMEM((lev, s, s), BF16),
        pltpu.VMEM((lb, r, nb), F32),
        pltpu.VMEM((lb - 1, nb, nb), BF16),
        pltpu.VMEM((lb - 1, 2 * nb, nb), BF16),
        pltpu.VMEM((lb - 1, r, nb), F32),
        pltpu.VMEM((lb, r, nb), BF16),
        pltpu.VMEM((lb, r + lev * s, nb), BF16),
        pltpu.VMEM((lb, r, nb), F32),
        pltpu.VMEM((lev, s, s), BF16),
        pltpu.VMEM((lev, s, s), BF16),
        pltpu.VMEM((lev, s, s), BF16),
        pltpu.VMEM((lev, 2 * nrep, w, s), F32),
        pltpu.VMEM((lev, 2, r // 2, s), F32),
        pltpu.VMEM((lev, r // 2, s), F32),
        pltpu.VMEM((lev, nrep, w, s), F32),
        pltpu.VMEM((lev, nrep - 1, w, s), F32),
        pltpu.VMEM((lev - 1, lev, w, s), F32),
        pltpu.VMEM((lev - 1, lev, w, s), F32),
        pltpu.VMEM((lev, 2 * nrep, w, s), F32),
        pltpu.VMEM((lb, nb, r), F32),
        pltpu.VMEM((lev, s, r), F32),
    ] + [
        pltpu.SemaphoreType.DMA(shape)
        for shape in (
            (4 + 4 * lev,),
            (lev,),
            (lev,),
            (lev, nrep - 1),
            (lev, nrep - 1),
            (lev - 1, lev),
            (lev - 1, lev),
            (lev, nrep - 1),
            (lev, nrep - 1),
            (lev,),
            (lev,),
            (lev + lb // 4,),
        )
    ]
    local, sep = pl.pallas_call(
        functools.partial(body, nleaf, nrep),
        out_shape=(
            jax.ShapeDtypeStruct((lb, nb, r), F32),
            jax.ShapeDtypeStruct((lev, s, r), F32),
        ),
        in_specs=[pl.BlockSpec(memory_space=pltpu.SMEM)] + [any_spec] * 8,
        out_specs=(any_spec, any_spec),
        scratch_shapes=scratch,
        compiler_params=pltpu.CompilerParams(
            collective_id=0, has_side_effects=True, vmem_limit_bytes=48 * 2**20
        ),
        name="wiener_solve",
    )(
        local_parent[0, 0],
        local_right[0, 0].reshape(lb, nb, r),
        local_inverse[0, 0],
        local_below[0, 0],
        local_coupling[0, 0],
        separator_right,
        separator_inverse,
        separator_lower,
        parent_coupling,
    )
    return local.reshape(1, 1, rows, r), sep[None]


def solution(mesh):
    in_specs = (
        P("leaf", "rep", None, None),
        P("leaf", "rep", None, None, None),
        P("leaf", "rep", None, None, None),
        P("leaf", "rep", None),
        P("leaf", "rep", None, None, None),
        P(),
        P(),
        P(),
        P(),
    )
    out_specs = (P("leaf", "rep", None, None), P("leaf", None, None, None))
    return jax.shard_map(
        functools.partial(on_device, mesh.shape["leaf"], mesh.shape["rep"]),
        mesh=mesh,
        in_specs=in_specs,
        out_specs=out_specs,
        check_vma=False,
    )
```

```python
import functools

import jax
import jax.numpy as jnp
from jax import lax
from jax.experimental import pallas as pl
from jax.experimental.pallas import tpu as pltpu
from jax.sharding import PartitionSpec as P

F32 = jnp.float32
BF16 = jnp.bfloat16
MESH = pl.DeviceIdType.MESH


def nn(a, b):
    return jnp.dot(a, b, preferred_element_type=F32)


def nt(a, b):
    return lax.dot_general(a, b, (((1,), (1,)), ((), ())), preferred_element_type=F32)


def body(
    nleaf,
    nrep,
    par_hbm,
    right_hbm,
    inv_hbm,
    below_hbm,
    coup_hbm,
    sright_hbm,
    sinv_hbm,
    slow_hbm,
    pcoup_hbm,
    out_hbm,
    sep_hbm,
    par,
    right,
    inv,
    below,
    coup,
    sright,
    sinv,
    slow,
    pcoup,
    invc,
    ctr,
    mfw,
    wbw,
    pj,
    x,
    eb,
    s0,
    tmat,
    qmat,
    umat,
    srt,
    part,
    pc,
    ph,
    zr,
    rem,
    lr,
    sol,
    out_v,
    sep_v,
    in_sem,
    core_s,
    core_r,
    z_s,
    z_r,
    l_s,
    l_r,
    g_s,
    g_r,
    gc_s,
    gc_r,
    out_sem,
):
    lev = coup.shape[0]
    lb = inv.shape[0]
    nb = inv.shape[1]
    s = coup.shape[1]
    sb = s // nb
    leaf = lax.axis_index("leaf")
    rep = lax.axis_index("rep")
    core = lax.rem(leaf, 2)
    mate = leaf + 1 - 2 * core

    def other_rep(d):
        return lax.rem(rep + d, nrep)

    def other_leaf(height):
        step = 1 << (height - 1)
        bit = lax.rem(leaf // step, 2)
        return leaf + step - 2 * step * bit

    numbers = [(nleaf >> h) - 1 + leaf // (1 << h) for h in range(1, lev + 1)]

    loads = [
        pltpu.make_async_copy(inv_hbm, inv, in_sem.at[0]),
        pltpu.make_async_copy(right_hbm, right, in_sem.at[1]),
        pltpu.make_async_copy(below_hbm, below, in_sem.at[2]),
        pltpu.make_async_copy(coup_hbm, coup, in_sem.at[3]),
        pltpu.make_async_copy(par_hbm, par, in_sem.at[4]),
    ]
    sep_loads = []
    for h in range(lev):
        n = numbers[h]
        base = 5 + 4 * h
        sep_loads.append(pltpu.make_async_copy(sinv_hbm.at[n], sinv.at[h], in_sem.at[base]))
        sep_loads.append(pltpu.make_async_copy(slow_hbm.at[n], slow.at[h], in_sem.at[base + 1]))
        sep_loads.append(pltpu.make_async_copy(sright_hbm.at[n], sright.at[h], in_sem.at[base + 2]))
        if h < lev - 1:
            sep_loads.append(
                pltpu.make_async_copy(pcoup_hbm.at[n - 1], pcoup.at[h], in_sem.at[base + 3])
            )
    for c in loads + sep_loads:
        c.start()

    barrier = pltpu.get_barrier_semaphore()
    peers = [(mate, rep)]
    peers += [(leaf, other_rep(d)) for d in range(1, nrep)]
    peers += [(other_leaf(h), rep) for h in range(2, lev + 1)]
    for peer in peers:
        pl.semaphore_signal(barrier, inc=1, device_id=peer, device_id_type=MESH)

    npair = lb // 2
    wide = 2 * nb
    loads[0].wait()
    loads[2].wait()
    loads[4].wait()
    for q in range(npair):
        lo, hi = 2 * q, 2 * q + 1
        inside = jnp.where(par[lo] == hi, 1.0, 0.0)
        scaled = nn(below[lo], inv[lo])
        corner = (-inside * nn(inv[hi], scaled.astype(BF16))).astype(BF16)
        zero = jnp.zeros((nb, nb), BF16)
        wbw[q, :nb, :nb] = inv[lo]
        wbw[q, :nb, nb:] = zero
        wbw[q, nb:wide, :nb] = corner
        wbw[q, nb:wide, nb:] = inv[hi]
        invc[lo, :nb] = inv[lo]
        invc[lo, nb:] = corner
        invc[hi, :nb] = zero
        invc[hi, nb:] = inv[hi]
        if q < npair - 1:
            wbw[q, wide : wide + nb, :nb] = ((inside - 1.0) * scaled).astype(BF16)
            wbw[q, wide : wide + nb, nb:] = zero

    for b in range(lb - 2):
        mfw[b] = nn(invc[par[b]], below[b]).astype(BF16)
    loads[1].wait()
    for q in range(npair):
        rows = jnp.concatenate([right[2 * q].T, right[2 * q + 1].T], axis=1)
        ctr[q] = nt(rows.astype(BF16), wbw[q, :wide])
    for q in range(npair):
        acc = ctr[q]
        for b in range(2 * q):
            hit = (par[b] >= 2 * q) & (par[b] <= 2 * q + 1)
            acc = acc - jnp.where(hit, 1.0, 0.0) * pj[b]
        fb = acc.astype(BF16)
        x[q] = fb
        if q < npair - 1:
            pj[2 * q] = nt(fb[:, :nb], mfw[2 * q])
            pj[2 * q + 1] = nt(fb[:, nb:], mfw[2 * q + 1])

    pl.semaphore_wait(barrier, len(peers))
    loads[3].wait()
    fwd = jnp.concatenate([x[q] for q in range(npair)], axis=1)
    half = part.shape[2]
    core_copies = []
    for h in range(lev):
        prod = nt(fwd, coup[h])
        part[h, 0] = prod[:half]
        part[h, 1] = prod[half:]
        c = pltpu.make_async_remote_copy(
            src_ref=part.at[h, 1 - core],
            dst_ref=pc.at[h],
            send_sem=core_s.at[h],
            recv_sem=core_r.at[h],
            device_id=(mate, rep),
            device_id_type=MESH,
        )
        c.start()
        core_copies.append(c)

    for c in sep_loads:
        c.wait()

    def prepare(h):
        def low(i, j):
            return slow[h, i * nb : (i + 1) * nb, j * nb : (j + 1) * nb]

        t = {}
        for j in range(sb):
            t[j, j] = sinv[h, j]
            for i in range(j + 1, sb):
                total = nn(low(i, j), t[j, j])
                for m in range(j + 1, i):
                    total = total + nn(low(i, m), t[m, j])
                t[i, j] = (-nn(sinv[h, i], total.astype(BF16))).astype(BF16)
        for i in range(sb):
            for j in range(sb):
                block = t[i, j] if i >= j else jnp.zeros((nb, nb), BF16)
                tmat[h, i * nb : (i + 1) * nb, j * nb : (j + 1) * nb] = block
        full = tmat[h]
        umat[h] = lax.dot_general(
            full, full, (((0,), (0,)), ((), ())), preferred_element_type=F32
        ).astype(BF16)
        if h < lev - 1:
            qmat[h] = nn(pcoup[h], full).astype(BF16)
        srt[h] = sright[h].T.reshape(srt.shape[1:])

    prepare(0)

    rep_copies = []
    for h in range(lev):
        core_copies[h].wait()
        ph[h] = part[h, core].reshape(ph.shape[1:]) + pc[h].reshape(ph.shape[1:])
        row = []
        for d in range(1, nrep):
            c = pltpu.make_async_remote_copy(
                src_ref=ph.at[h, other_rep(d)],
                dst_ref=zr.at[h, d - 1],
                send_sem=z_s.at[h, d - 1],
                recv_sem=z_r.at[h, d - 1],
                device_id=(leaf, other_rep(d)),
                device_id_type=MESH,
            )
            c.start()
            row.append(c)
        rep_copies.append(row)

    for h in range(1, lev):
        prepare(h)

    for q in range(npair - 1):
        wbw[q, wide + nb :] = (-nn(below[2 * q + 1], wbw[q, nb:wide])).astype(BF16)

    r = x.shape[1]

    def back_step(q):
        lanes = slice(q * wide, (q + 1) * wide)
        for g in range(lev + 1):
            if g == 0:
                rows = slice(0, r)
                mine = x[q]
            else:
                rows = slice(r + (g - 1) * s, r + g * s)
                mine = coup[g - 1, :, lanes]
            if q == npair - 1:
                value = nn(mine, wbw[q, :wide])
            else:
                one = eb[jnp.maximum(par[2 * q], 2 * q + 2), rows]
                two = eb[par[2 * q + 1], rows]
                value = nn(jnp.concatenate([mine, one, two], axis=1), wbw[q])
            eb[2 * q, rows] = value[:, :nb].astype(BF16)
            eb[2 * q + 1, rows] = value[:, nb:].astype(BF16)
            if g == 0:
                s0[q] = value

    steps = list(range(npair - 1, -1, -1))
    first = (npair * 5) // 8
    rest = npair - first
    for q in steps[:first]:
        back_step(q)
    steps = steps[first:]
    share = -(-rest // max(lev - 1, 1))

    slot = core * nrep + rep
    leaf_copies = {}

    def send_leaf(height, j):
        c = pltpu.make_async_remote_copy(
            src_ref=rem.at[height - 2, j],
            dst_ref=lr.at[height - 2, j],
            send_sem=l_s.at[height - 2, j],
            recv_sem=l_r.at[height - 2, j],
            device_id=(other_leaf(height), rep),
            device_id_type=MESH,
        )
        c.start()
        leaf_copies[height, j] = c

    def total_of(h):
        total = ph[h, rep]
        for c in rep_copies[h]:
            c.wait()
        for d in range(1, nrep):
            total = total + zr[h, d - 1]
        return total

    residues = []
    for height in range(1, lev + 1):
        h = height - 1
        if height == 1:
            now = total_of(0)
        else:
            leaf_copies[height, h].wait()
            now = rem[height - 2, h] + lr[height - 2, h]
        residue = (srt[h, slot] - now).astype(BF16)
        residues.append(residue)
        if height < lev:
            up = nt(residue, qmat[h])
            for j in range(height, lev):
                if height == 1:
                    value = total_of(j)
                else:
                    leaf_copies[height, j].wait()
                    value = rem[height - 2, j] + lr[height - 2, j]
                if j == height:
                    value = value + up
                rem[height - 1, j] = value
                send_leaf(height + 1, j)
            for q in steps[:share]:
                back_step(q)
            steps = steps[share:]

    gather_copies = []
    above = None
    for h in range(lev - 1, -1, -1):
        value = nn(residues[h], umat[h])
        if above is not None:
            value = value - nn(above, qmat[h])
        above = value.astype(BF16)
        sol[h, slot] = value
        row = []
        for d in range(1, nrep):
            c = pltpu.make_async_remote_copy(
                src_ref=sol.at[h, slot],
                dst_ref=sol.at[h, slot],
                send_sem=g_s.at[h, d - 1],
                recv_sem=g_r.at[h, d - 1],
                device_id=(leaf, other_rep(d)),
                device_id_type=MESH,
            )
            c.start()
            row.append(c)
        gather_copies.append(row)
    mate_copies = {}
    out_copies = []

    def share_with_mate(h):
        for c in gather_copies[lev - 1 - h]:
            c.wait()
        c = pltpu.make_async_remote_copy(
            src_ref=sol.at[h, pl.ds(core * nrep, nrep)],
            dst_ref=sol.at[h, pl.ds(core * nrep, nrep)],
            send_sem=gc_s.at[h],
            recv_sem=gc_r.at[h],
            device_id=(mate, rep),
            device_id_type=MESH,
        )
        c.start()
        mate_copies[h] = c

    def whole_solution(h):
        mate_copies[h].wait()
        return sol[h].reshape(r, s)

    def write_separator(h, whole):
        sep_v[h] = whole.T
        c = pltpu.make_async_copy(sep_v.at[h], sep_hbm.at[h], out_sem.at[h])
        c.start()
        out_copies.append(c)

    def weights(q, rows):
        return jnp.concatenate([eb[2 * q, rows], eb[2 * q + 1, rows]], axis=1)

    for h in range(lev - 1, 0, -1):
        share_with_mate(h)
    uppers = [whole_solution(h) for h in range(1, lev)]
    upper = jnp.concatenate([u.astype(BF16) for u in uppers], axis=1)
    rows = slice(r + s, r + lev * s)
    for q in range(npair):
        s0[q] = s0[q] - nn(upper, weights(q, rows))
    share_with_mate(0)
    for h in range(1, lev):
        write_separator(h, uppers[h - 1])
    lowest = whole_solution(0)
    lower = lowest.astype(BF16)
    rows = slice(r, r + s)
    for q in range(npair):
        value = s0[q] - nn(lower, weights(q, rows))
        out_v[2 * q] = value[:, :nb].T
        out_v[2 * q + 1] = value[:, nb:].T
        if q % 2 == 1:
            part_q = pl.ds(2 * q - 2, 4)
            c = pltpu.make_async_copy(
                out_v.at[part_q], out_hbm.at[part_q], out_sem.at[lev + q // 2]
            )
            c.start()
            out_copies.append(c)
    write_separator(0, lowest)
    for c in out_copies:
        c.wait()


def hand_out(local_in, sep_in, local_out, sep_out, sem):
    first = pltpu.make_async_copy(local_in, local_out, sem.at[0])
    second = pltpu.make_async_copy(sep_in, sep_out, sem.at[1])
    first.start()
    second.start()
    first.wait()
    second.wait()


def on_device(
    nleaf,
    nrep,
    local_right,
    local_inverse,
    local_below,
    local_parent,
    local_coupling,
    separator_right,
    separator_inverse,
    separator_lower,
    parent_coupling,
):
    _, _, lev, s, rows = local_coupling.shape
    lb, nb = local_inverse.shape[2:4]
    r = local_right.shape[3]
    w = r // (2 * nrep)
    sb = s // nb
    any_spec = pl.BlockSpec(memory_space=pl.ANY)
    hbm_spec = pl.BlockSpec(memory_space=pltpu.HBM)
    scratch = [
        pltpu.SMEM((lb - 1,), jnp.int32),
        pltpu.VMEM((lb, nb, r), F32),
        pltpu.VMEM((lb, nb, nb), BF16),
        pltpu.VMEM((lb - 1, nb, nb), BF16),
        pltpu.VMEM((lev, s, rows), BF16),
        pltpu.VMEM((lev, s, r), F32),
        pltpu.VMEM((lev, sb, nb, nb), BF16),
        pltpu.VMEM((lev, s, s), BF16),
        pltpu.VMEM((lev, s, s), BF16),
        pltpu.VMEM((lb, 2 * nb, nb), BF16),
        pltpu.VMEM((lb // 2, r, 2 * nb), F32),
        pltpu.VMEM((lb - 2, 2 * nb, nb), BF16),
        pltpu.VMEM((lb // 2, 4 * nb, 2 * nb), BF16),
        pltpu.VMEM((lb - 2, r, 2 * nb), F32),
        pltpu.VMEM((lb // 2, r, 2 * nb), BF16),
        pltpu.VMEM((lb, r + lev * s, nb), BF16),
        pltpu.VMEM((lb // 2, r, 2 * nb), F32),
        pltpu.VMEM((lev, s, s), BF16),
        pltpu.VMEM((lev, s, s), BF16),
        pltpu.VMEM((lev, s, s), BF16),
        pltpu.VMEM((lev, 2 * nrep, w, s), F32),
        pltpu.VMEM((lev, 2, r // 2, s), F32),
        pltpu.VMEM((lev, r // 2, s), F32),
        pltpu.VMEM((lev, nrep, w, s), F32),
        pltpu.VMEM((lev, nrep - 1, w, s), F32),
        pltpu.VMEM((lev - 1, lev, w, s), F32),
        pltpu.VMEM((lev - 1, lev, w, s), F32),
        pltpu.VMEM((lev, 2 * nrep, w, s), F32),
        pltpu.VMEM((lb, nb, r), F32),
        pltpu.VMEM((lev, s, r), F32),
    ] + [
        pltpu.SemaphoreType.DMA(shape)
        for shape in (
            (5 + 4 * lev,),
            (lev,),
            (lev,),
            (lev, nrep - 1),
            (lev, nrep - 1),
            (lev - 1, lev),
            (lev - 1, lev),
            (lev, nrep - 1),
            (lev, nrep - 1),
            (lev,),
            (lev,),
            (lev + lb // 4,),
        )
    ]
    local, sep = pl.pallas_call(
        functools.partial(body, nleaf, nrep),
        out_shape=(
            jax.ShapeDtypeStruct((lb, nb, r), F32),
            jax.ShapeDtypeStruct((lev, s, r), F32),
        ),
        in_specs=[hbm_spec] * 9,
        out_specs=(any_spec, any_spec),
        scratch_shapes=scratch,
        compiler_params=pltpu.CompilerParams(
            collective_id=0, has_side_effects=True, vmem_limit_bytes=63 * 2**20
        ),
        name="wiener_solve",
    )(
        local_parent[0, 0],
        local_right[0, 0].reshape(lb, nb, r),
        local_inverse[0, 0],
        local_below[0, 0],
        local_coupling[0, 0],
        separator_right,
        separator_inverse,
        separator_lower,
        parent_coupling,
    )
    local, sep = pl.pallas_call(
        hand_out,
        out_shape=(
            jax.ShapeDtypeStruct((lb, nb, r), F32),
            jax.ShapeDtypeStruct((lev, s, r), F32),
        ),
        in_specs=[any_spec] * 2,
        out_specs=(hbm_spec, hbm_spec),
        scratch_shapes=[pltpu.SemaphoreType.DMA((2,))],
        compiler_params=pltpu.CompilerParams(vmem_limit_bytes=63 * 2**20),
        name="hand_out",
    )(local, sep)
    return local.reshape(1, 1, rows, r), sep[None]


def solution(mesh):
    in_specs = (
        P("leaf", "rep", None, None),
        P("leaf", "rep", None, None, None),
        P("leaf", "rep", None, None, None),
        P("leaf", "rep", None),
        P("leaf", "rep", None, None, None),
        P(),
        P(),
        P(),
        P(),
    )
    out_specs = (P("leaf", "rep", None, None), P("leaf", None, None, None))
    return jax.shard_map(
        functools.partial(on_device, mesh.shape["leaf"], mesh.shape["rep"]),
        mesh=mesh,
        in_specs=in_specs,
        out_specs=out_specs,
        check_vma=False,
    )
```

```python
import functools

import jax
import jax.numpy as jnp
from jax import lax
from jax.experimental import pallas as pl
from jax.experimental.pallas import tpu as pltpu
from jax.sharding import PartitionSpec as P

F32 = jnp.float32
BF16 = jnp.bfloat16
MESH = pl.DeviceIdType.MESH


def nn(a, b):
    return jnp.dot(a, b, preferred_element_type=F32)


def nt(a, b):
    return lax.dot_general(a, b, (((1,), (1,)), ((), ())), preferred_element_type=F32)


def body(
    nleaf,
    nrep,
    par_hbm,
    right_hbm,
    inv_hbm,
    below_hbm,
    coup_hbm,
    sright_hbm,
    sinv_hbm,
    slow_hbm,
    pcoup_hbm,
    out_hbm,
    sep_hbm,
    par,
    right,
    inv,
    below,
    coup,
    sright,
    sinv,
    slow,
    pcoup,
    invc,
    ctr,
    mfw,
    wbw,
    pj,
    x,
    eb,
    s0,
    tmat,
    qmat,
    umat,
    srt,
    part,
    pc,
    ph,
    zr,
    rem,
    lr,
    sol,
    out_v,
    sep_v,
    in_sem,
    core_s,
    core_r,
    z_s,
    z_r,
    l_s,
    l_r,
    g_s,
    g_r,
    gc_s,
    gc_r,
    out_sem,
):
    lev = coup.shape[0]
    lb = inv.shape[0]
    nb = inv.shape[1]
    s = coup.shape[1]
    sb = s // nb
    leaf = lax.axis_index("leaf")
    rep = lax.axis_index("rep")
    core = lax.rem(leaf, 2)
    mate = leaf + 1 - 2 * core

    def other_rep(d):
        return lax.rem(rep + d, nrep)

    def other_leaf(height):
        step = 1 << (height - 1)
        bit = lax.rem(leaf // step, 2)
        return leaf + step - 2 * step * bit

    numbers = [(nleaf >> h) - 1 + leaf // (1 << h) for h in range(1, lev + 1)]

    loads = [
        pltpu.make_async_copy(inv_hbm, inv, in_sem.at[0]),
        pltpu.make_async_copy(right_hbm, right, in_sem.at[1]),
        pltpu.make_async_copy(below_hbm, below, in_sem.at[2]),
        pltpu.make_async_copy(coup_hbm, coup, in_sem.at[3]),
        pltpu.make_async_copy(par_hbm, par, in_sem.at[4]),
    ]
    sep_loads = []
    for h in range(lev):
        n = numbers[h]
        base = 5 + 4 * h
        sep_loads.append(pltpu.make_async_copy(sinv_hbm.at[n], sinv.at[h], in_sem.at[base]))
        sep_loads.append(pltpu.make_async_copy(slow_hbm.at[n], slow.at[h], in_sem.at[base + 1]))
        sep_loads.append(pltpu.make_async_copy(sright_hbm.at[n], sright.at[h], in_sem.at[base + 2]))
        if h < lev - 1:
            sep_loads.append(
                pltpu.make_async_copy(pcoup_hbm.at[n - 1], pcoup.at[h], in_sem.at[base + 3])
            )
    for c in loads + sep_loads:
        c.start()

    barrier = pltpu.get_barrier_semaphore()
    peers = [(mate, rep)]
    peers += [(leaf, other_rep(d)) for d in range(1, nrep)]
    peers += [(other_leaf(h), rep) for h in range(2, lev + 1)]
    for peer in peers:
        pl.semaphore_signal(barrier, inc=1, device_id=peer, device_id_type=MESH)

    npair = lb // 2
    wide = 2 * nb
    loads[0].wait()
    loads[2].wait()
    loads[4].wait()
    for q in range(npair):
        lo, hi = 2 * q, 2 * q + 1
        inside = jnp.where(par[lo] == hi, 1.0, 0.0)
        scaled = nn(below[lo], inv[lo])
        corner = (-inside * nn(inv[hi], scaled.astype(BF16))).astype(BF16)
        zero = jnp.zeros((nb, nb), BF16)
        wbw[q, :nb, :nb] = inv[lo]
        wbw[q, :nb, nb:] = zero
        wbw[q, nb:wide, :nb] = corner
        wbw[q, nb:wide, nb:] = inv[hi]
        invc[lo, :nb] = inv[lo]
        invc[lo, nb:] = corner
        invc[hi, :nb] = zero
        invc[hi, nb:] = inv[hi]
        if q < npair - 1:
            wbw[q, wide : wide + nb, :nb] = ((inside - 1.0) * scaled).astype(BF16)
            wbw[q, wide : wide + nb, nb:] = zero

    for b in range(lb - 2):
        mfw[b] = nn(invc[par[b]], below[b]).astype(BF16)
    loads[1].wait()
    for q in range(npair):
        rows = jnp.concatenate([right[2 * q].T, right[2 * q + 1].T], axis=1)
        ctr[q] = nt(rows.astype(BF16), wbw[q, :wide])
    for q in range(npair):
        acc = ctr[q]
        for b in range(2 * q):
            hit = (par[b] >= 2 * q) & (par[b] <= 2 * q + 1)
            acc = acc - jnp.where(hit, 1.0, 0.0) * pj[b]
        fb = acc.astype(BF16)
        x[q] = fb
        if q < npair - 1:
            pj[2 * q] = nt(fb[:, :nb], mfw[2 * q])
            pj[2 * q + 1] = nt(fb[:, nb:], mfw[2 * q + 1])

    pl.semaphore_wait(barrier, len(peers))
    loads[3].wait()
    fwd = jnp.concatenate([x[q] for q in range(npair)], axis=1)
    half = part.shape[2]
    core_copies = []
    for h in range(lev):
        prod = nt(fwd, coup[h])
        part[h, 0] = prod[:half]
        part[h, 1] = prod[half:]
        c = pltpu.make_async_remote_copy(
            src_ref=part.at[h, 1 - core],
            dst_ref=pc.at[h],
            send_sem=core_s.at[h],
            recv_sem=core_r.at[h],
            device_id=(mate, rep),
            device_id_type=MESH,
        )
        c.start()
        core_copies.append(c)

    for c in sep_loads:
        c.wait()

    def prepare(h):
        def low(i, j):
            return slow[h, i * nb : (i + 1) * nb, j * nb : (j + 1) * nb]

        t = {}
        for j in range(sb):
            t[j, j] = sinv[h, j]
            for i in range(j + 1, sb):
                total = nn(low(i, j), t[j, j])
                for m in range(j + 1, i):
                    total = total + nn(low(i, m), t[m, j])
                t[i, j] = (-nn(sinv[h, i], total.astype(BF16))).astype(BF16)
        for i in range(sb):
            for j in range(sb):
                block = t[i, j] if i >= j else jnp.zeros((nb, nb), BF16)
                tmat[h, i * nb : (i + 1) * nb, j * nb : (j + 1) * nb] = block
        full = tmat[h]
        umat[h] = lax.dot_general(
            full, full, (((0,), (0,)), ((), ())), preferred_element_type=F32
        ).astype(BF16)
        if h < lev - 1:
            qmat[h] = nn(pcoup[h], full).astype(BF16)
        srt[h] = sright[h].T.reshape(srt.shape[1:])

    prepare(0)

    rep_copies = []
    for h in range(lev):
        core_copies[h].wait()
        ph[h] = part[h, core].reshape(ph.shape[1:]) + pc[h].reshape(ph.shape[1:])
        row = []
        for d in range(1, nrep):
            c = pltpu.make_async_remote_copy(
                src_ref=ph.at[h, other_rep(d)],
                dst_ref=zr.at[h, d - 1],
                send_sem=z_s.at[h, d - 1],
                recv_sem=z_r.at[h, d - 1],
                device_id=(leaf, other_rep(d)),
                device_id_type=MESH,
            )
            c.start()
            row.append(c)
        rep_copies.append(row)

    for h in range(1, lev):
        prepare(h)

    for q in range(npair - 1):
        wbw[q, wide + nb :] = (-nn(below[2 * q + 1], wbw[q, nb:wide])).astype(BF16)

    r = x.shape[1]

    def back_step(q):
        lanes = slice(q * wide, (q + 1) * wide)
        for g in range(lev + 1):
            if g == 0:
                rows = slice(0, r)
                mine = x[q]
            else:
                rows = slice(r + (g - 1) * s, r + g * s)
                mine = coup[g - 1, :, lanes]
            if q == npair - 1:
                value = nn(mine, wbw[q, :wide])
            else:
                one = eb[jnp.maximum(par[2 * q], 2 * q + 2), rows]
                two = eb[par[2 * q + 1], rows]
                value = nn(jnp.concatenate([mine, one, two], axis=1), wbw[q])
            eb[2 * q, rows] = value[:, :nb].astype(BF16)
            eb[2 * q + 1, rows] = value[:, nb:].astype(BF16)
            if g == 0:
                s0[q] = value

    steps = list(range(npair - 1, -1, -1))

    def spend(count):
        for q in steps[:count]:
            back_step(q)
        del steps[:count]

    spend(3)

    slot = core * nrep + rep
    leaf_copies = {}

    def send_leaf(height, j):
        c = pltpu.make_async_remote_copy(
            src_ref=rem.at[height - 2, j],
            dst_ref=lr.at[height - 2, j],
            send_sem=l_s.at[height - 2, j],
            recv_sem=l_r.at[height - 2, j],
            device_id=(other_leaf(height), rep),
            device_id_type=MESH,
        )
        c.start()
        leaf_copies[height, j] = c

    def total_of(h):
        total = ph[h, rep]
        for c in rep_copies[h]:
            c.wait()
        for d in range(1, nrep):
            total = total + zr[h, d - 1]
        return total

    gather_copies = {}
    mate_copies = {}
    out_copies = []

    def gather(h, residue):
        sol[h, slot] = residue
        row = []
        for d in range(1, nrep):
            c = pltpu.make_async_remote_copy(
                src_ref=sol.at[h, slot],
                dst_ref=sol.at[h, slot],
                send_sem=g_s.at[h, d - 1],
                recv_sem=g_r.at[h, d - 1],
                device_id=(leaf, other_rep(d)),
                device_id_type=MESH,
            )
            c.start()
            row.append(c)
        gather_copies[h] = row

    def share_with_mate(h):
        for c in gather_copies[h]:
            c.wait()
        c = pltpu.make_async_remote_copy(
            src_ref=sol.at[h, pl.ds(core * nrep, nrep)],
            dst_ref=sol.at[h, pl.ds(core * nrep, nrep)],
            send_sem=gc_s.at[h],
            recv_sem=gc_r.at[h],
            device_id=(mate, rep),
            device_id_type=MESH,
        )
        c.start()
        mate_copies[h] = c

    for height in range(1, lev + 1):
        h = height - 1
        if height == 1:
            now = total_of(0)
        else:
            leaf_copies[height, h].wait()
            now = rem[height - 2, h] + lr[height - 2, h]
        residue = srt[h, slot] - now
        gather(h, residue)
        if height < lev:
            up = nt(residue.astype(BF16), qmat[h])
            for j in range(height, lev):
                if height == 1:
                    spend(1)
                    value = total_of(j)
                else:
                    leaf_copies[height, j].wait()
                    value = rem[height - 2, j] + lr[height - 2, j]
                if j == height:
                    value = value + up
                rem[height - 1, j] = value
                send_leaf(height + 1, j)
            spend(2)
            if height > 1:
                share_with_mate(height - 2)
    spend(npair)
    share_with_mate(lev - 2)

    def level_rows(h):
        return slice(r + h * s, r + (h + 1) * s)

    def weights(q, h):
        rows = level_rows(h)
        return jnp.concatenate([eb[2 * q, rows], eb[2 * q + 1, rows]], axis=1)

    def fold(h):
        for q in range(npair):
            value = weights(q, h + 1).astype(F32) - nn(qmat[h], weights(q, h))
            eb[2 * q, level_rows(h + 1)] = value[:, :nb].astype(BF16)
            eb[2 * q + 1, level_rows(h + 1)] = value[:, nb:].astype(BF16)

    def spread(h):
        mate_copies[h].wait()
        return nn(sol[h].reshape(r, s).astype(BF16), umat[h])

    spreads = []
    for h in range(lev - 1):
        fold(h)
        spreads.append(spread(h))
        gb = spreads[h].astype(BF16)
        for q in range(npair):
            s0[q] = s0[q] - nn(gb, weights(q, h))
    share_with_mate(lev - 1)
    spreads.append(spread(lev - 1))
    gb = spreads[lev - 1].astype(BF16)
    for q in range(npair):
        value = s0[q] - nn(gb, weights(q, lev - 1))
        out_v[2 * q] = value[:, :nb].T
        out_v[2 * q + 1] = value[:, nb:].T
        if q % 2 == 1:
            part_q = pl.ds(2 * q - 2, 4)
            c = pltpu.make_async_copy(
                out_v.at[part_q], out_hbm.at[part_q], out_sem.at[lev + q // 2]
            )
            c.start()
            out_copies.append(c)
    whole = None
    for h in range(lev - 1, -1, -1):
        if whole is None:
            whole = spreads[h]
        else:
            whole = spreads[h] - nn(whole.astype(BF16), qmat[h])
        sep_v[h] = whole.T
        c = pltpu.make_async_copy(sep_v.at[h], sep_hbm.at[h], out_sem.at[h])
        c.start()
        out_copies.append(c)
    for c in out_copies:
        c.wait()


def hand_out(local_in, sep_in, local_out, sep_out, local_v, sep_v, in_sem, out_sem):
    loads, stores = [], []
    chunk = local_v.shape[0] // 4
    for i in range(4):
        part = pl.ds(i * chunk, chunk)
        loads.append(
            pltpu.make_async_copy(local_in.at[part], local_v.at[part], in_sem.at[i])
        )
        stores.append(
            pltpu.make_async_copy(local_v.at[part], local_out.at[part], out_sem.at[i])
        )
    loads.append(pltpu.make_async_copy(sep_in, sep_v, in_sem.at[4]))
    stores.append(pltpu.make_async_copy(sep_v, sep_out, out_sem.at[4]))
    for load in loads:
        load.start()
    for load, store in zip(loads, stores):
        load.wait()
        store.start()
    for store in stores:
        store.wait()


def on_device(
    nleaf,
    nrep,
    local_right,
    local_inverse,
    local_below,
    local_parent,
    local_coupling,
    separator_right,
    separator_inverse,
    separator_lower,
    parent_coupling,
):
    _, _, lev, s, rows = local_coupling.shape
    lb, nb = local_inverse.shape[2:4]
    r = local_right.shape[3]
    w = r // (2 * nrep)
    sb = s // nb
    any_spec = pl.BlockSpec(memory_space=pl.ANY)
    hbm_spec = pl.BlockSpec(memory_space=pltpu.HBM)
    scratch = [
        pltpu.SMEM((lb - 1,), jnp.int32),
        pltpu.VMEM((lb, nb, r), F32),
        pltpu.VMEM((lb, nb, nb), BF16),
        pltpu.VMEM((lb - 1, nb, nb), BF16),
        pltpu.VMEM((lev, s, rows), BF16),
        pltpu.VMEM((lev, s, r), F32),
        pltpu.VMEM((lev, sb, nb, nb), BF16),
        pltpu.VMEM((lev, s, s), BF16),
        pltpu.VMEM((lev, s, s), BF16),
        pltpu.VMEM((lb, 2 * nb, nb), BF16),
        pltpu.VMEM((lb // 2, r, 2 * nb), F32),
        pltpu.VMEM((lb - 2, 2 * nb, nb), BF16),
        pltpu.VMEM((lb // 2, 4 * nb, 2 * nb), BF16),
        pltpu.VMEM((lb - 2, r, 2 * nb), F32),
        pltpu.VMEM((lb // 2, r, 2 * nb), BF16),
        pltpu.VMEM((lb, r + lev * s, nb), BF16),
        pltpu.VMEM((lb // 2, r, 2 * nb), F32),
        pltpu.VMEM((lev, s, s), BF16),
        pltpu.VMEM((lev, s, s), BF16),
        pltpu.VMEM((lev, s, s), BF16),
        pltpu.VMEM((lev, 2 * nrep, w, s), F32),
        pltpu.VMEM((lev, 2, r // 2, s), F32),
        pltpu.VMEM((lev, r // 2, s), F32),
        pltpu.VMEM((lev, nrep, w, s), F32),
        pltpu.VMEM((lev, nrep - 1, w, s), F32),
        pltpu.VMEM((lev - 1, lev, w, s), F32),
        pltpu.VMEM((lev - 1, lev, w, s), F32),
        pltpu.VMEM((lev, 2 * nrep, w, s), F32),
        pltpu.VMEM((lb, nb, r), F32),
        pltpu.VMEM((lev, s, r), F32),
    ] + [
        pltpu.SemaphoreType.DMA(shape)
        for shape in (
            (5 + 4 * lev,),
            (lev,),
            (lev,),
            (lev, nrep - 1),
            (lev, nrep - 1),
            (lev - 1, lev),
            (lev - 1, lev),
            (lev, nrep - 1),
            (lev, nrep - 1),
            (lev,),
            (lev,),
            (lev + lb // 4,),
        )
    ]
    local, sep = pl.pallas_call(
        functools.partial(body, nleaf, nrep),
        out_shape=(
            jax.ShapeDtypeStruct((lb, nb, r), F32),
            jax.ShapeDtypeStruct((lev, s, r), F32),
        ),
        in_specs=[hbm_spec] * 9,
        out_specs=(any_spec, any_spec),
        scratch_shapes=scratch,
        compiler_params=pltpu.CompilerParams(
            collective_id=0, has_side_effects=True, vmem_limit_bytes=63 * 2**20
        ),
        name="wiener_solve",
    )(
        local_parent[0, 0],
        local_right[0, 0].reshape(lb, nb, r),
        local_inverse[0, 0],
        local_below[0, 0],
        local_coupling[0, 0],
        separator_right,
        separator_inverse,
        separator_lower,
        parent_coupling,
    )
    local, sep = pl.pallas_call(
        hand_out,
        out_shape=(
            jax.ShapeDtypeStruct((lb, nb, r), F32),
            jax.ShapeDtypeStruct((lev, s, r), F32),
        ),
        in_specs=[any_spec] * 2,
        out_specs=(hbm_spec, hbm_spec),
        scratch_shapes=[
            pltpu.VMEM((lb, nb, r), F32),
            pltpu.VMEM((lev, s, r), F32),
            pltpu.SemaphoreType.DMA((5,)),
            pltpu.SemaphoreType.DMA((5,)),
        ],
        compiler_params=pltpu.CompilerParams(vmem_limit_bytes=63 * 2**20),
        name="hand_out",
    )(local, sep)
    return local.reshape(1, 1, rows, r), sep[None]


def solution(mesh):
    in_specs = (
        P("leaf", "rep", None, None),
        P("leaf", "rep", None, None, None),
        P("leaf", "rep", None, None, None),
        P("leaf", "rep", None),
        P("leaf", "rep", None, None, None),
        P(),
        P(),
        P(),
        P(),
    )
    out_specs = (P("leaf", "rep", None, None), P("leaf", None, None, None))
    return jax.shard_map(
        functools.partial(on_device, mesh.shape["leaf"], mesh.shape["rep"]),
        mesh=mesh,
        in_specs=in_specs,
        out_specs=out_specs,
        check_vma=False,
    )
```

```python
import functools

import jax
import jax.numpy as jnp
from jax import lax
from jax.experimental import pallas as pl
from jax.experimental.pallas import tpu as pltpu
from jax.sharding import PartitionSpec as P

F32 = jnp.float32
BF16 = jnp.bfloat16
MESH = pl.DeviceIdType.MESH


def nn(a, b):
    return jnp.dot(a, b, preferred_element_type=F32)


def nt(a, b):
    return lax.dot_general(a, b, (((1,), (1,)), ((), ())), preferred_element_type=F32)


def body(
    nleaf,
    nrep,
    par_hbm,
    right_hbm,
    inv_hbm,
    below_hbm,
    coup_hbm,
    sright_hbm,
    sinv_hbm,
    slow_hbm,
    pcoup_hbm,
    out_hbm,
    sep_hbm,
    par,
    right,
    inv,
    below,
    coup,
    sright,
    sinv,
    slow,
    pcoup,
    invc,
    ctr,
    mfw,
    wbw,
    pj,
    x,
    eb,
    s0,
    tmat,
    qmat,
    umat,
    srt,
    part,
    pc,
    ph,
    zr,
    rem,
    lr,
    sol,
    out_v,
    sep_v,
    in_sem,
    core_s,
    core_r,
    z_s,
    z_r,
    l_s,
    l_r,
    g_s,
    g_r,
    gc_s,
    gc_r,
    out_sem,
):
    lev = coup.shape[0]
    lb = inv.shape[0]
    nb = inv.shape[1]
    s = coup.shape[1]
    sb = s // nb
    leaf = lax.axis_index("leaf")
    rep = lax.axis_index("rep")
    core = lax.rem(leaf, 2)
    mate = leaf + 1 - 2 * core

    def other_rep(d):
        return lax.rem(rep + d, nrep)

    def other_leaf(height):
        step = 1 << (height - 1)
        bit = lax.rem(leaf // step, 2)
        return leaf + step - 2 * step * bit

    numbers = [(nleaf >> h) - 1 + leaf // (1 << h) for h in range(1, lev + 1)]

    loads = [
        pltpu.make_async_copy(inv_hbm, inv, in_sem.at[0]),
        pltpu.make_async_copy(right_hbm, right, in_sem.at[1]),
        pltpu.make_async_copy(below_hbm, below, in_sem.at[2]),
        pltpu.make_async_copy(coup_hbm, coup, in_sem.at[3]),
        pltpu.make_async_copy(par_hbm, par, in_sem.at[4]),
    ]
    sep_loads = []
    for h in range(lev):
        n = numbers[h]
        base = 5 + 4 * h
        sep_loads.append(pltpu.make_async_copy(sinv_hbm.at[n], sinv.at[h], in_sem.at[base]))
        sep_loads.append(pltpu.make_async_copy(slow_hbm.at[n], slow.at[h], in_sem.at[base + 1]))
        sep_loads.append(pltpu.make_async_copy(sright_hbm.at[n], sright.at[h], in_sem.at[base + 2]))
        if h < lev - 1:
            sep_loads.append(
                pltpu.make_async_copy(pcoup_hbm.at[n - 1], pcoup.at[h], in_sem.at[base + 3])
            )
    for c in loads + sep_loads:
        c.start()

    barrier = pltpu.get_barrier_semaphore()
    peers = [(mate, rep)]
    peers += [(leaf, other_rep(d)) for d in range(1, nrep)]
    peers += [(other_leaf(h), rep) for h in range(2, lev + 1)]
    for peer in peers:
        pl.semaphore_signal(barrier, inc=1, device_id=peer, device_id_type=MESH)

    npair = lb // 2
    wide = 2 * nb
    loads[0].wait()
    loads[2].wait()
    loads[4].wait()
    for q in range(npair):
        lo, hi = 2 * q, 2 * q + 1
        inside = jnp.where(par[lo] == hi, 1.0, 0.0)
        scaled = nn(below[lo], inv[lo])
        corner = (-inside * nn(inv[hi], scaled.astype(BF16))).astype(BF16)
        zero = jnp.zeros((nb, nb), BF16)
        wbw[q, :nb, :nb] = inv[lo]
        wbw[q, :nb, nb:] = zero
        wbw[q, nb:wide, :nb] = corner
        wbw[q, nb:wide, nb:] = inv[hi]
        invc[lo, :nb] = inv[lo]
        invc[lo, nb:] = corner
        invc[hi, :nb] = zero
        invc[hi, nb:] = inv[hi]
        if q < npair - 1:
            wbw[q, wide : wide + nb, :nb] = ((inside - 1.0) * scaled).astype(BF16)
            wbw[q, wide : wide + nb, nb:] = zero

    for b in range(lb - 2):
        mfw[b] = nn(invc[par[b]], below[b]).astype(BF16)
    loads[1].wait()
    for q in range(npair):
        rows = jnp.concatenate([right[2 * q].T, right[2 * q + 1].T], axis=1)
        ctr[q] = nt(rows.astype(BF16), wbw[q, :wide])
    for q in range(npair):
        acc = ctr[q]
        for b in range(2 * q):
            hit = (par[b] >= 2 * q) & (par[b] <= 2 * q + 1)
            acc = acc - jnp.where(hit, 1.0, 0.0) * pj[b]
        fb = acc.astype(BF16)
        x[q] = fb
        if q < npair - 1:
            pj[2 * q] = nt(fb[:, :nb], mfw[2 * q])
            pj[2 * q + 1] = nt(fb[:, nb:], mfw[2 * q + 1])

    pl.semaphore_wait(barrier, len(peers))
    loads[3].wait()
    fwd = jnp.concatenate([x[q] for q in range(npair)], axis=1)
    half = part.shape[2]
    core_copies = []
    rep_copies = []

    def send_core(h):
        prod = nt(fwd, coup[h])
        part[h, 0] = prod[:half]
        part[h, 1] = prod[half:]
        c = pltpu.make_async_remote_copy(
            src_ref=part.at[h, 1 - core],
            dst_ref=pc.at[h],
            send_sem=core_s.at[h],
            recv_sem=core_r.at[h],
            device_id=(mate, rep),
            device_id_type=MESH,
        )
        c.start()
        core_copies.append(c)

    def send_rep(h):
        core_copies[h].wait()
        ph[h] = part[h, core].reshape(ph.shape[1:]) + pc[h].reshape(ph.shape[1:])
        row = []
        for d in range(1, nrep):
            c = pltpu.make_async_remote_copy(
                src_ref=ph.at[h, other_rep(d)],
                dst_ref=zr.at[h, d - 1],
                send_sem=z_s.at[h, d - 1],
                recv_sem=z_r.at[h, d - 1],
                device_id=(leaf, other_rep(d)),
                device_id_type=MESH,
            )
            c.start()
            row.append(c)
        rep_copies.append(row)

    send_core(0)
    for h in range(1, lev):
        send_core(h)
        send_rep(h - 1)

    for c in sep_loads:
        c.wait()
    levels = range(lev)
    t = {}

    def low(h, i, j):
        return slow[h, i * nb : (i + 1) * nb, j * nb : (j + 1) * nb]

    for h in levels:
        for i in range(sb):
            t[h, i, i] = sinv[h, i]
    for gap in range(1, sb):
        for j in range(sb - gap):
            i = j + gap
            totals = [
                sum(nn(low(h, i, m), t[h, m, j]) for m in range(j, i)) for h in levels
            ]
            for h in levels:
                t[h, i, j] = (-nn(sinv[h, i], totals[h].astype(BF16))).astype(BF16)
    for h in levels:
        for i in range(sb):
            for j in range(sb):
                block = t[h, i, j] if i >= j else jnp.zeros((nb, nb), BF16)
                tmat[h, i * nb : (i + 1) * nb, j * nb : (j + 1) * nb] = block
        if h < lev - 1:
            qmat[h] = nn(pcoup[h], tmat[h]).astype(BF16)
        srt[h] = sright[h].T.reshape(srt.shape[1:])
    send_rep(lev - 1)

    for q in range(npair - 1):
        wbw[q, wide + nb :] = (-nn(below[2 * q + 1], wbw[q, nb:wide])).astype(BF16)

    r = x.shape[1]

    def back_step(q):
        lanes = slice(q * wide, (q + 1) * wide)
        for g in range(lev + 1):
            if g == 0:
                rows = slice(0, r)
                mine = x[q]
            else:
                rows = slice(r + (g - 1) * s, r + g * s)
                mine = coup[g - 1, :, lanes]
            if q == npair - 1:
                value = nn(mine, wbw[q, :wide])
            else:
                one = eb[jnp.maximum(par[2 * q], 2 * q + 2), rows]
                two = eb[par[2 * q + 1], rows]
                value = nn(jnp.concatenate([mine, one, two], axis=1), wbw[q])
            eb[2 * q, rows] = value[:, :nb].astype(BF16)
            eb[2 * q + 1, rows] = value[:, nb:].astype(BF16)
            if g == 0:
                s0[q] = value

    steps = list(range(npair - 1, -1, -1))

    def spend(count):
        for q in steps[:count]:
            back_step(q)
        del steps[:count]

    spend(2)

    slot = core * nrep + rep
    leaf_copies = {}

    def send_leaf(height, j):
        c = pltpu.make_async_remote_copy(
            src_ref=rem.at[height - 2, j],
            dst_ref=lr.at[height - 2, j],
            send_sem=l_s.at[height - 2, j],
            recv_sem=l_r.at[height - 2, j],
            device_id=(other_leaf(height), rep),
            device_id_type=MESH,
        )
        c.start()
        leaf_copies[height, j] = c

    def total_of(h):
        total = ph[h, rep]
        for c in rep_copies[h]:
            c.wait()
        for d in range(1, nrep):
            total = total + zr[h, d - 1]
        return total

    gather_copies = {}
    mate_copies = {}
    out_copies = []

    def gather(h, residue):
        sol[h, slot] = residue
        row = []
        for d in range(1, nrep):
            c = pltpu.make_async_remote_copy(
                src_ref=sol.at[h, slot],
                dst_ref=sol.at[h, slot],
                send_sem=g_s.at[h, d - 1],
                recv_sem=g_r.at[h, d - 1],
                device_id=(leaf, other_rep(d)),
                device_id_type=MESH,
            )
            c.start()
            row.append(c)
        gather_copies[h] = row

    def share_with_mate(h):
        for c in gather_copies[h]:
            c.wait()
        c = pltpu.make_async_remote_copy(
            src_ref=sol.at[h, pl.ds(core * nrep, nrep)],
            dst_ref=sol.at[h, pl.ds(core * nrep, nrep)],
            send_sem=gc_s.at[h],
            recv_sem=gc_r.at[h],
            device_id=(mate, rep),
            device_id_type=MESH,
        )
        c.start()
        mate_copies[h] = c

    for height in range(1, lev + 1):
        h = height - 1
        if height == 1:
            now = total_of(0)
        else:
            leaf_copies[height, h].wait()
            now = rem[height - 2, h] + lr[height - 2, h]
        residue = srt[h, slot] - now
        gather(h, residue)
        if height < lev:
            up = nt(residue.astype(BF16), qmat[h])
            for j in range(height, lev):
                if height == 1:
                    spend(1)
                    value = total_of(j)
                else:
                    leaf_copies[height, j].wait()
                    value = rem[height - 2, j] + lr[height - 2, j]
                if j == height:
                    value = value + up
                rem[height - 1, j] = value
                send_leaf(height + 1, j)
            spend(2)
            if height > 1:
                share_with_mate(height - 2)
    spend(npair)
    share_with_mate(lev - 2)
    for h in levels:
        full = tmat[h]
        umat[h] = lax.dot_general(
            full, full, (((0,), (0,)), ((), ())), preferred_element_type=F32
        ).astype(BF16)

    def level_rows(h):
        return slice(r + h * s, r + (h + 1) * s)

    def weights(q, h):
        rows = level_rows(h)
        return jnp.concatenate([eb[2 * q, rows], eb[2 * q + 1, rows]], axis=1)

    def fold(h):
        for q in range(npair):
            value = weights(q, h + 1).astype(F32) - nn(qmat[h], weights(q, h))
            eb[2 * q, level_rows(h + 1)] = value[:, :nb].astype(BF16)
            eb[2 * q + 1, level_rows(h + 1)] = value[:, nb:].astype(BF16)

    def spread(h):
        mate_copies[h].wait()
        return nn(sol[h].reshape(r, s).astype(BF16), umat[h])

    spreads = []
    for h in range(lev - 1):
        fold(h)
        if h == lev - 2:
            share_with_mate(lev - 1)
        spreads.append(spread(h))
        gb = spreads[h].astype(BF16)
        for q in range(npair):
            s0[q] = s0[q] - nn(gb, weights(q, h))
    spreads.append(spread(lev - 1))
    gb = spreads[lev - 1].astype(BF16)
    for q in range(npair):
        value = s0[q] - nn(gb, weights(q, lev - 1))
        out_v[2 * q] = value[:, :nb].T
        out_v[2 * q + 1] = value[:, nb:].T
        if q % 2 == 1:
            part_q = pl.ds(2 * q - 2, 4)
            c = pltpu.make_async_copy(
                out_v.at[part_q], out_hbm.at[part_q], out_sem.at[lev + q // 2]
            )
            c.start()
            out_copies.append(c)
    whole = None
    for h in range(lev - 1, -1, -1):
        if whole is None:
            whole = spreads[h]
        else:
            whole = spreads[h] - nn(whole.astype(BF16), qmat[h])
        sep_v[h] = whole.T
        c = pltpu.make_async_copy(sep_v.at[h], sep_hbm.at[h], out_sem.at[h])
        c.start()
        out_copies.append(c)
    for c in out_copies:
        c.wait()


def hand_out(local_in, sep_in, local_out, sep_out, local_v, sep_v, in_sem, out_sem):
    loads, stores = [], []
    chunk = local_v.shape[0] // 4
    for i in range(4):
        part = pl.ds(i * chunk, chunk)
        loads.append(
            pltpu.make_async_copy(local_in.at[part], local_v.at[part], in_sem.at[i])
        )
        stores.append(
            pltpu.make_async_copy(local_v.at[part], local_out.at[part], out_sem.at[i])
        )
    loads.append(pltpu.make_async_copy(sep_in, sep_v, in_sem.at[4]))
    stores.append(pltpu.make_async_copy(sep_v, sep_out, out_sem.at[4]))
    for load in loads:
        load.start()
    for load, store in zip(loads, stores):
        load.wait()
        store.start()
    for store in stores:
        store.wait()


def on_device(
    nleaf,
    nrep,
    local_right,
    local_inverse,
    local_below,
    local_parent,
    local_coupling,
    separator_right,
    separator_inverse,
    separator_lower,
    parent_coupling,
):
    _, _, lev, s, rows = local_coupling.shape
    lb, nb = local_inverse.shape[2:4]
    r = local_right.shape[3]
    w = r // (2 * nrep)
    sb = s // nb
    any_spec = pl.BlockSpec(memory_space=pl.ANY)
    hbm_spec = pl.BlockSpec(memory_space=pltpu.HBM)
    scratch = [
        pltpu.SMEM((lb - 1,), jnp.int32),
        pltpu.VMEM((lb, nb, r), F32),
        pltpu.VMEM((lb, nb, nb), BF16),
        pltpu.VMEM((lb - 1, nb, nb), BF16),
        pltpu.VMEM((lev, s, rows), BF16),
        pltpu.VMEM((lev, s, r), F32),
        pltpu.VMEM((lev, sb, nb, nb), BF16),
        pltpu.VMEM((lev, s, s), BF16),
        pltpu.VMEM((lev, s, s), BF16),
        pltpu.VMEM((lb, 2 * nb, nb), BF16),
        pltpu.VMEM((lb // 2, r, 2 * nb), F32),
        pltpu.VMEM((lb - 2, 2 * nb, nb), BF16),
        pltpu.VMEM((lb // 2, 4 * nb, 2 * nb), BF16),
        pltpu.VMEM((lb - 2, r, 2 * nb), F32),
        pltpu.VMEM((lb // 2, r, 2 * nb), BF16),
        pltpu.VMEM((lb, r + lev * s, nb), BF16),
        pltpu.VMEM((lb // 2, r, 2 * nb), F32),
        pltpu.VMEM((lev, s, s), BF16),
        pltpu.VMEM((lev, s, s), BF16),
        pltpu.VMEM((lev, s, s), BF16),
        pltpu.VMEM((lev, 2 * nrep, w, s), F32),
        pltpu.VMEM((lev, 2, r // 2, s), F32),
        pltpu.VMEM((lev, r // 2, s), F32),
        pltpu.VMEM((lev, nrep, w, s), F32),
        pltpu.VMEM((lev, nrep - 1, w, s), F32),
        pltpu.VMEM((lev - 1, lev, w, s), F32),
        pltpu.VMEM((lev - 1, lev, w, s), F32),
        pltpu.VMEM((lev, 2 * nrep, w, s), F32),
        pltpu.VMEM((lb, nb, r), F32),
        pltpu.VMEM((lev, s, r), F32),
    ] + [
        pltpu.SemaphoreType.DMA(shape)
        for shape in (
            (5 + 4 * lev,),
            (lev,),
            (lev,),
            (lev, nrep - 1),
            (lev, nrep - 1),
            (lev - 1, lev),
            (lev - 1, lev),
            (lev, nrep - 1),
            (lev, nrep - 1),
            (lev,),
            (lev,),
            (lev + lb // 4,),
        )
    ]
    local, sep = pl.pallas_call(
        functools.partial(body, nleaf, nrep),
        out_shape=(
            jax.ShapeDtypeStruct((lb, nb, r), F32),
            jax.ShapeDtypeStruct((lev, s, r), F32),
        ),
        in_specs=[hbm_spec] * 9,
        out_specs=(any_spec, any_spec),
        scratch_shapes=scratch,
        compiler_params=pltpu.CompilerParams(
            collective_id=0, has_side_effects=True, vmem_limit_bytes=63 * 2**20
        ),
        name="wiener_solve",
    )(
        local_parent[0, 0],
        local_right[0, 0].reshape(lb, nb, r),
        local_inverse[0, 0],
        local_below[0, 0],
        local_coupling[0, 0],
        separator_right,
        separator_inverse,
        separator_lower,
        parent_coupling,
    )
    local, sep = pl.pallas_call(
        hand_out,
        out_shape=(
            jax.ShapeDtypeStruct((lb, nb, r), F32),
            jax.ShapeDtypeStruct((lev, s, r), F32),
        ),
        in_specs=[any_spec] * 2,
        out_specs=(hbm_spec, hbm_spec),
        scratch_shapes=[
            pltpu.VMEM((lb, nb, r), F32),
            pltpu.VMEM((lev, s, r), F32),
            pltpu.SemaphoreType.DMA((5,)),
            pltpu.SemaphoreType.DMA((5,)),
        ],
        compiler_params=pltpu.CompilerParams(vmem_limit_bytes=63 * 2**20),
        name="hand_out",
    )(local, sep)
    return local.reshape(1, 1, rows, r), sep[None]


def solution(mesh):
    in_specs = (
        P("leaf", "rep", None, None),
        P("leaf", "rep", None, None, None),
        P("leaf", "rep", None, None, None),
        P("leaf", "rep", None),
        P("leaf", "rep", None, None, None),
        P(),
        P(),
        P(),
        P(),
    )
    out_specs = (P("leaf", "rep", None, None), P("leaf", None, None, None))
    return jax.shard_map(
        functools.partial(on_device, mesh.shape["leaf"], mesh.shape["rep"]),
        mesh=mesh,
        in_specs=in_specs,
        out_specs=out_specs,
        check_vma=False,
    )
```
